32 devices in a mesh: section: 8 (over z, x), expert: 4 (over y, core).
Axes of the slice: x: 2, y: 2, z: 4, core: 2. Of those that a mesh axis runs over, the one named last changes fastest.
Arguments:
- tokens: bfloat16 [8, 768, 1024], P('section', 'expert'), may hold values from -6 to 6
- out_grad: bfloat16 [8, 768, 1024], P('section', 'expert'), may hold values from -6 to 6
- expert_ids: int32 [8, 768, 2], P('section', 'expert'), may hold values from 0 to 3, all different within a row; in each aligned block of 192 rows (0 to 191, 192 to 383, ..., all dimensions but the last counted through in order) at most 192 rows name the same one
- gate_weights: float32 [8, 768, 2], P('section', 'expert'), may hold values from 0.2 to 1
- w_gate: bfloat16 [8, 4, 1024, 256], P('section', 'expert'), may hold values from -0.1875 to 0.1875
- w_up: bfloat16 [8, 4, 1024, 256], P('section', 'expert'), may hold values from -0.1875 to 0.1875
- w_down: bfloat16 [8, 4, 256, 1024], P('section', 'expert'), may hold values from -0.25 to 0.25
Outputs:
- token_grad: bfloat16 [8, 768, 1024], P('section', 'expert')
- grad_gate: bfloat16 [8, 4, 1024, 256], P('section', 'expert')
- grad_up: bfloat16 [8, 4, 1024, 256], P('section', 'expert')
- grad_down: bfloat16 [8, 4, 256, 1024], P('section', 'expert')
The draws below stay inside these ranges and needn't reach their ends.
Inputs may be any that keep to these rules, and one draw needn't show every extreme that they name: `expert_ids`: each token names 2 different experts. Among the 192 tokens of one device (aligned blocks of rows of one section) no expert is named by more than 192 (token, choice) pairs, a bound that some block reaches.
All inputs are finite; a program needn't handle non-finite values.
Results may differ from the reference program's by a relative error of at most 0.009.
Values may be sent and summed in bfloat16 or wider, within the bound.
A program may use at most 64 MiB of HBM per device.

```python
import math
import jax
import jax.numpy as jnp
import numpy as np
from jax import lax

D = 1024
H = 512
TOPK = 2
TOK_DEV = 192
HH = 256
EXPERTS = 4
TOKENS = 768
CAP = 192
N_SECTION = 8
N_EXPERT = 4


def block_levels(rng, dims, shards, smallest, largest):
    def one(position, parts):
        draws = jax.random.uniform(jax.random.fold_in(jax.random.fold_in(rng, 6), position), (parts,), jnp.float32, smallest / len(shards), largest / len(shards))
        return jnp.repeat(jnp.exp(draws), dims[position] // parts).reshape((-1,) + (1,) * (len(dims) - position - 1))

    loudness = one(*shards[0])
    for cut in shards[1:]:
        loudness = loudness * one(*cut)
    return loudness


def deal_out(key, own, number, rows, amount, top, most, slope):
    ranking = jax.random.permutation(key, amount)
    crowded, common = portions_of(amount, rows * top, most, slope, True), portions_of(amount, rows * top, most, slope, False)
    places = jnp.arange(amount)

    def named(lengths, offset_by):
        used = int((lengths > 0).sum())
        fixed = max(1, used // 4)
        passed = fixed + (places - fixed + offset_by * (used - fixed)) % max(1, amount - fixed)
        return jnp.zeros((amount,), jnp.int32).at[ranking[jnp.where(places < fixed, places, passed)]].set(jnp.asarray(lengths, jnp.int32))

    lengths = jnp.where(number % 4 == 0, named(crowded, number // 4), named(common, number - number // 4 - 1))
    mixed = jax.random.permutation(jax.random.fold_in(own, 3), amount)
    donor, receiver = mixed[0:amount // 2 * 2:2], mixed[1:amount // 2 * 2:2]
    room = jnp.minimum(lengths[donor] - 1, most - lengths[receiver]) // 2
    room = jnp.where((donor == ranking[0]) | (receiver == ranking[0]) | (lengths[receiver] == 0), 0, jnp.maximum(room, 0))
    passed = jax.random.randint(jax.random.fold_in(own, 4), (amount // 2,), 0, 1 << 20) % (room + 1)
    lengths = lengths.at[donor].add(-passed).at[receiver].add(passed)
    items = jnp.searchsorted(jnp.cumsum(lengths), jnp.arange(rows * top), side="right").astype(jnp.int32)
    grid = items.reshape(top, rows).T
    grid = grid[jax.random.permutation(jax.random.fold_in(own, 1), rows)]
    offset_by = jax.random.randint(jax.random.fold_in(own, 2), (rows, 1), 0, top)
    return jnp.take_along_axis(grid, (jnp.arange(top)[None, :] + offset_by) % top, axis=1)


def portions_of(number_of, total, reach, lean, full):
    portions = [(1 << 20) // math.isqrt(grade ** lean) + 1 for grade in range(1, number_of + 1)]
    largest = reach if full else min(reach, max(-(-total // number_of), total * portions[0] // sum(portions)))
    least = 1 if total - largest >= number_of - 1 else 0
    counts, spare = [largest] + [least] * (number_of - 1), total - largest - least * (number_of - 1)
    while spare > 0:
        candidates = [i for i in range(1, number_of) if counts[i] < largest] or [i for i in range(1, number_of) if counts[i] < reach]
        mass, budget = sum([portions[i] for i in candidates]), spare
        for i in candidates:
            more = min(reach - counts[i], max(1, budget * portions[i] // mass), spare)
            counts[i] = counts[i] + more
            spare = spare - more
    return np.array(counts)


def noise(own_key, dims, scale, most, split=(), kind=jnp.bfloat16):
    level = block_levels(own_key, dims, split, -0.22, 0.18) if split else 1.0
    values = jax.random.normal(own_key, dims, jnp.float32) * scale * level
    return jnp.minimum(jnp.maximum(values, -most), most).astype(kind)


def setup_inputs(seed: int = 0) -> dict:
    keys = jax.random.split(jax.random.key(seed), 8)
    tokens = noise(keys[0], (N_SECTION, TOKENS, D), 1.0, 6.0, ((0, 8), (1, 4)))
    out_grad = noise(keys[1], (N_SECTION, TOKENS, D), 1.0, 6.0, ((0, 8), (1, 4)))
    expert_ids_keys = jax.random.split(jax.random.fold_in(keys[2], 1), N_SECTION * TOKENS // TOK_DEV)
    expert_ids_turns = jax.random.permutation(jax.random.fold_in(keys[2], 3), N_SECTION * TOKENS // TOK_DEV)
    expert_ids = jax.vmap(lambda own, number: deal_out(jax.random.fold_in(keys[2], 2), own, number, TOK_DEV, EXPERTS, TOPK, CAP, 2))(expert_ids_keys, expert_ids_turns).reshape((N_SECTION, TOKENS, TOPK))
    gate_weights = jnp.clip(0.2 + 0.8 * jax.random.uniform(keys[3], (N_SECTION, TOKENS, TOPK), jnp.float32) ** block_levels(keys[3], (N_SECTION, TOKENS, TOPK), ((0, 8), (1, 4)), -0.2, 0.2), 0.2, 1.0)
    w_gate = noise(keys[4], (N_SECTION, EXPERTS, D, HH), D ** -0.5, 0.1875, ((0, 8), (1, 4)))
    w_up = noise(keys[5], (N_SECTION, EXPERTS, D, HH), D ** -0.5, 0.1875, ((0, 8), (1, 4)))
    w_down = noise(keys[6], (N_SECTION, EXPERTS, HH, D), H ** -0.5, 0.25, ((0, 8), (1, 4)))
    return dict(tokens=tokens, out_grad=out_grad, expert_ids=expert_ids, gate_weights=gate_weights, w_gate=w_gate, w_up=w_up, w_down=w_down)


def make_slots(ids, gates, inputs, grads, cap, experts):
    tok, topk = ids.shape
    width = inputs.shape[1]
    count = tok * topk
    flat = ids.reshape(count)
    onehot = (flat[:, None] == jnp.arange(experts, dtype=jnp.int32)[None, :]).astype(jnp.int32)
    before = jnp.cumsum(onehot, axis=0) - onehot
    rank = lax.optimization_barrier(jnp.sum(before * onehot, axis=1)).astype(jnp.int32)
    slot = (flat * cap + rank).astype(jnp.int32)
    source = jnp.full((experts * cap,), count, jnp.int32).at[slot].set(jnp.arange(count, dtype=jnp.int32))
    token = (source // topk).astype(jnp.int32)
    padded_in = jnp.concatenate([inputs, jnp.zeros((1, width), inputs.dtype)], axis=0)
    scaled = (gates.astype(jnp.float32)[:, :, None] * grads.astype(jnp.float32)[:, None, :]).astype(jnp.bfloat16)
    padded_grad = jnp.concatenate([scaled.reshape(count, width), jnp.zeros((1, width), jnp.bfloat16)], axis=0)
    slot_in = padded_in[token].reshape(experts, cap, width)
    slot_grad = padded_grad[source].reshape(experts, cap, width)
    live = (source < count).reshape(experts, cap)
    return (slot_in, slot_grad, live, slot)

def unslot(slot_rows, slot, tok, topk):
    width = slot_rows.shape[-1]
    picked = slot_rows[slot].astype(jnp.float32).reshape(tok, topk, width)
    return lax.optimization_barrier(jnp.sum(picked, axis=1)).astype(jnp.bfloat16)

def expert_grads(rows_in, rows_grad, gate_w, up_w, down_w):
    contract_last = (((1,), (1,)), ((), ()))
    contract_rows = (((0,), (0,)), ((), ()))
    gate_pre = jnp.dot(rows_in, gate_w, preferred_element_type=jnp.float32)
    up_pre = jnp.dot(rows_in, up_w, preferred_element_type=jnp.float32)
    sigmoid_g = jax.nn.sigmoid(gate_pre)
    swish_val = gate_pre * sigmoid_g
    act = (swish_val * up_pre).astype(jnp.bfloat16)
    act_grad = lax.dot_general(rows_grad, down_w, contract_last, preferred_element_type=jnp.float32)
    gate_grad = (act_grad * up_pre * sigmoid_g * (1.0 + gate_pre * (1.0 - sigmoid_g))).astype(jnp.bfloat16)
    up_grad = (act_grad * swish_val).astype(jnp.bfloat16)
    pair_grad = lax.dot_general(gate_grad, gate_w, contract_last, preferred_element_type=jnp.float32)
    pair_grad = pair_grad + lax.dot_general(up_grad, up_w, contract_last, preferred_element_type=jnp.float32)
    grad_g = lax.dot_general(rows_in, gate_grad, contract_rows, preferred_element_type=jnp.float32)
    grad_u = lax.dot_general(rows_in, up_grad, contract_rows, preferred_element_type=jnp.float32)
    grad_d = lax.dot_general(act, rows_grad, contract_rows, preferred_element_type=jnp.float32)
    return (pair_grad, grad_g, grad_u, grad_d)

def reference(tokens, out_grad, expert_ids, gate_weights, w_gate, w_up, w_down):
    pairs = N_SECTION // 2
    blocks = 2 * N_EXPERT
    scale = 1.0 / math.sqrt(2 * TOPK * TOK_DEV)

    def one_pair(index):
        other = index + pairs

        def both(array):
            return jnp.stack([array[index], array[other]])
        x_all = both(tokens).reshape(blocks, TOK_DEV, D)
        dy_all = both(out_grad).reshape(blocks, TOK_DEV, D)
        ids_all = both(expert_ids).reshape(blocks, TOK_DEV, TOPK)
        gw_all = both(gate_weights).reshape(blocks, TOK_DEV, TOPK)

        def slots_of(ids, gates, inputs, grads):
            return make_slots(ids, gates, inputs, grads, CAP, EXPERTS)
        slot_in, slot_grad, live, slot = jax.vmap(slots_of)(ids_all, gw_all, x_all, dy_all)
        x_exp = jnp.transpose(slot_in, (1, 0, 2, 3)).reshape(EXPERTS, blocks * CAP, D)
        dy_exp = jnp.transpose(slot_grad, (1, 0, 2, 3)).reshape(EXPERTS, blocks * CAP, D)
        full_gate = jnp.concatenate([w_gate[index], w_gate[other]], axis=2)
        full_up = jnp.concatenate([w_up[index], w_up[other]], axis=2)
        full_down = jnp.concatenate([w_down[index], w_down[other]], axis=1)

        def per_expert(items):
            return expert_grads(items[0], items[1], items[2], items[3], items[4])
        pair_grad, grad_g, grad_u, grad_d = lax.map(per_expert, (x_exp, dy_exp, full_gate, full_up, full_down))
        back = pair_grad.astype(jnp.bfloat16).reshape(EXPERTS, blocks, CAP, D)
        back = jnp.transpose(back, (1, 0, 2, 3)).reshape(blocks, EXPERTS * CAP, D)

        def unslot_one(rows, where_to):
            return unslot(rows, where_to, TOK_DEV, TOPK)
        token_part = jax.vmap(unslot_one)(back, slot).reshape(2, TOKENS, D)
        grad_g = (grad_g * scale).astype(jnp.bfloat16)
        grad_u = (grad_u * scale).astype(jnp.bfloat16)
        grad_d = (grad_d * scale).astype(jnp.bfloat16)
        gate_two = jnp.stack([grad_g[:, :, :HH], grad_g[:, :, HH:]])
        up_two = jnp.stack([grad_u[:, :, :HH], grad_u[:, :, HH:]])
        down_two = jnp.stack([grad_d[:, :HH, :], grad_d[:, HH:, :]])
        return (token_part, gate_two, up_two, down_two)
    token_all, gate_all, up_all, down_all = lax.map(one_pair, jnp.arange(pairs, dtype=jnp.int32))

    def arrange(array):
        moved = jnp.swapaxes(array, 0, 1)
        return moved.reshape((N_SECTION,) + moved.shape[2:])
    return (arrange(token_all), arrange(gate_all), arrange(up_all), arrange(down_all))
```

```python
import functools
import math

import jax
import jax.numpy as jnp
from jax import lax
from jax.experimental import pallas as pl
from jax.experimental.pallas import tpu as pltpu
from jax.sharding import PartitionSpec as P

MESH = pl.DeviceIdType.MESH
CHUNKS = 2
SLOTS = 4


def partner(value, axis, bit):
    mask = 2**bit
    pairs = [(source, source ^ mask) for source in range(lax.axis_size(axis))]
    return lax.ppermute(value, axis, pairs)


def make_slots(ids, gates, inputs, grads, cap, experts):
    tok, topk = ids.shape
    width = inputs.shape[1]
    count = tok * topk
    flat = ids.reshape(count)
    place = jnp.arange(count, dtype=jnp.int32)
    earlier = (flat[:, None] == flat[None, :]) & (place[None, :] < place[:, None])
    rank = jnp.sum(earlier.astype(jnp.int32), axis=1)
    slot = flat * cap + rank
    source = (
        jnp.full((experts * cap,), count, jnp.int32)
        .at[slot]
        .set(jnp.arange(count, dtype=jnp.int32))
    )
    token = source // topk
    padded_in = jnp.concatenate([inputs, jnp.zeros((1, width), inputs.dtype)], axis=0)
    scaled = (gates[:, :, None] * grads.astype(jnp.float32)[:, None, :]).astype(jnp.bfloat16)
    padded_grad = jnp.concatenate(
        [scaled.reshape(count, width), jnp.zeros((1, width), jnp.bfloat16)], axis=0
    )
    slot_in = padded_in[token].reshape(experts, cap, width)
    slot_grad = padded_grad[source].reshape(experts, cap, width)
    live = (source < count).reshape(experts, cap)
    return (slot_in, slot_grad, live, slot)


def unslot(slot_rows, slot, tok, topk):
    width = slot_rows.shape[-1]
    picked = slot_rows[slot].astype(jnp.float32).reshape(tok, topk, width)
    return jnp.sum(picked, axis=1).astype(jnp.bfloat16)


def expert_grads(rows_in, rows_grad, gate_w, up_w, down_w):
    contract_last = (((1,), (1,)), ((), ()))
    contract_rows = (((0,), (0,)), ((), ()))
    gate_pre = jnp.dot(rows_in, gate_w, preferred_element_type=jnp.float32)
    up_pre = jnp.dot(rows_in, up_w, preferred_element_type=jnp.float32)
    sigmoid_g = jax.nn.sigmoid(gate_pre)
    swish_val = gate_pre * sigmoid_g
    act = (swish_val * up_pre).astype(jnp.bfloat16)
    act_grad = lax.dot_general(rows_grad, down_w, contract_last, preferred_element_type=jnp.float32)
    gate_grad = (act_grad * up_pre * sigmoid_g * (1.0 + gate_pre * (1.0 - sigmoid_g))).astype(
        jnp.bfloat16
    )
    up_grad = (act_grad * swish_val).astype(jnp.bfloat16)
    pair_grad = lax.dot_general(
        gate_grad, gate_w, contract_last, preferred_element_type=jnp.float32
    )
    pair_grad = pair_grad + lax.dot_general(
        up_grad, up_w, contract_last, preferred_element_type=jnp.float32
    )
    grad_g = lax.dot_general(rows_in, gate_grad, contract_rows, preferred_element_type=jnp.float32)
    grad_u = lax.dot_general(rows_in, up_grad, contract_rows, preferred_element_type=jnp.float32)
    grad_d = lax.dot_general(act, rows_grad, contract_rows, preferred_element_type=jnp.float32)
    return (pair_grad, grad_g, grad_u, grad_d)


def run_expert(rows_in, rows_grad, gate_w, up_w, down_w):
    return expert_grads(rows_in, rows_grad, gate_w, up_w, down_w)


def per_device(tokens, out_grad, expert_ids, gate_weights, w_gate, w_up, w_down):
    inputs = tokens[0]
    grads = out_grad[0]
    ids = expert_ids[0]
    gates = gate_weights[0]
    tok, topk = ids.shape
    width = inputs.shape[1]
    experts = lax.axis_size("expert")
    cap = 2 * topk * tok // experts
    scale = 1.0 / math.sqrt(2 * topk * tok)
    pair_bit = lax.axis_size("section").bit_length() - 2
    slot_in, slot_grad, live, slot = make_slots(ids, gates, inputs, grads, cap, experts)
    recv_in, recv_grad, recv_live = (
        lax.all_to_all(slot_in, "expert", split_axis=0, concat_axis=0, tiled=True),
        lax.all_to_all(slot_grad, "expert", split_axis=0, concat_axis=0, tiled=True),
        lax.all_to_all(
            live.astype(jnp.bfloat16), "expert", split_axis=0, concat_axis=0, tiled=True
        ),
    )
    rows = experts * cap
    recv_in = recv_in.reshape(rows, width)
    recv_grad = recv_grad.reshape(rows, width)
    recv_live = recv_live.reshape(rows)
    own_gate = w_gate[0, 0]
    own_up = w_up[0, 0]
    own_down = w_down[0, 0]
    half = own_gate.shape[1]
    other_gate, other_up, other_down = partner((own_gate, own_up, own_down), "section", pair_bit)
    full_gate = jnp.concatenate([own_gate, other_gate], axis=1)
    full_up = jnp.concatenate([own_up, other_up], axis=1)
    full_down = jnp.concatenate([own_down, other_down], axis=0)
    pair_grad, grad_g, grad_u, grad_d = run_expert(
        recv_in, recv_grad, full_gate, full_up, full_down
    )
    peer_g, peer_u, peer_d = (
        partner(grad_g[:, half:].astype(jnp.bfloat16), "section", pair_bit).astype(jnp.float32),
        partner(grad_u[:, half:].astype(jnp.bfloat16), "section", pair_bit).astype(jnp.float32),
        partner(grad_d[half:, :].astype(jnp.bfloat16), "section", pair_bit).astype(jnp.float32),
    )
    mine_g = grad_g[:, :half] + peer_g
    mine_u = grad_u[:, :half] + peer_u
    mine_d = grad_d[:half, :] + peer_d
    back_slots = pair_grad.astype(jnp.bfloat16).reshape(experts, cap, width)
    home_slots = lax.all_to_all(back_slots, "expert", split_axis=0, concat_axis=0, tiled=True)
    token_grad = unslot(home_slots.reshape(rows, width), slot, tok, topk)
    out_g = (mine_g * scale).astype(jnp.bfloat16)
    out_u = (mine_u * scale).astype(jnp.bfloat16)
    out_d = (mine_d * scale).astype(jnp.bfloat16)
    return (token_grad[None], out_g[None, None], out_u[None, None], out_d[None, None])


def gathered_kernel(
    sections, scale, x_hbm, dy_hbm, gates_hbm, wg_hbm, wu_hbm, wd_hbm,
    tok_out, g_out, u_out, d_out,
    rows, gates, w_gu, w_d, hidden, acts, part_send, part_recv, part_own,
    y_send, y_recv, z_send, z_recv, send_sem, recv_sem, local_sem,
):
    chunks, tr, width = rows.shape[1], rows.shape[4], rows.shape[5]
    half = w_d.shape[0]
    s, e = lax.axis_index("section"), lax.axis_index("expert")
    mirror = (lax.rem(s + sections // 2, sections), e)
    y_peer = (s, lax.rem(e + 2, 4))
    core_peer = (s, e + 1 - 2 * lax.rem(e, 2))

    local = []

    def bring(src, dst):
        copy = pltpu.make_async_copy(src, dst, local_sem.at[len(local)])
        copy.start()
        local.append(copy)

    for k in range(chunks):
        bring(x_hbm.at[pl.ds(k * tr, tr), :], rows.at[0, k, 0, 0])
        bring(dy_hbm.at[pl.ds(k * tr, tr), :], rows.at[0, k, 1, 0])
    bring(gates_hbm, gates.at[0, 0])
    own_copies = len(local)
    bring(wg_hbm, w_gu.at[:, pl.ds(0, half)])
    bring(wu_hbm, w_gu.at[:, pl.ds(half, half)])
    bring(wd_hbm, w_d)

    barrier = pltpu.get_barrier_semaphore()
    for peer in (mirror, y_peer, core_peer):
        pl.semaphore_signal(barrier, inc=1, device_id=peer, device_id_type=MESH)
    pl.semaphore_wait(barrier, 3)

    sent = []

    def send(src, dst, peer):
        n = len(sent)
        copy = pltpu.make_async_remote_copy(
            src_ref=src, dst_ref=dst, send_sem=send_sem.at[n], recv_sem=recv_sem.at[n],
            device_id=peer, device_id_type=MESH,
        )
        copy.start()
        sent.append(copy)
        return copy

    def send_block(side, k, slot, to_side, to_slot, peer):
        out = [send(rows.at[side, k, :, slot], rows.at[to_side, k, :, to_slot], peer)]
        if k == 0:
            out.append(send(gates.at[side, slot], gates.at[to_side, to_slot], peer))
        return out

    def arrived(copies):
        for copy in copies:
            copy.wait_recv()

    for copy in local[:own_copies]:
        copy.wait()
    by_z, by_y, by_core = {}, {}, {}
    for k in range(chunks):
        by_z[k] = send_block(0, k, 0, 1, 0, mirror)
        by_y[0, k] = send_block(0, k, 0, 0, 2, y_peer)
        by_core[0, k] = send_block(0, k, 0, 0, 1, core_peer)

    def from_y(side, k):
        arrived(by_y[side, k])
        by_core[side, k] += send_block(side, k, 2, side, 3, core_peer)

    def from_z(k):
        arrived(by_z[k])
        by_y[1, k] = send_block(1, k, 0, 1, 2, y_peer)
        by_core[1, k] = send_block(1, k, 0, 1, 1, core_peer)

    lanes = lax.broadcasted_iota(jnp.int32, (tr, gates.shape[2]), 1)
    contract_last = (((1,), (1,)), ((), ()))
    by_part, by_y_part, by_z_part = {}, {}, {}

    def stage(side, k):
        arrived(by_core[side, k])
        x = rows[side, k, 0].reshape(SLOTS * tr, width)
        dy = rows[side, k, 1].reshape(SLOTS * tr, width)
        columns = []
        for slot in range(SLOTS):
            turned = jnp.transpose(gates[side, slot])[k * tr : (k + 1) * tr, :]
            columns.append(
                jnp.sum(jnp.where(lanes == e, turned, 0.0), axis=1, keepdims=True)
            )
        weight = jnp.concatenate(columns, axis=0)
        pre = jnp.dot(x, w_gu[...], preferred_element_type=jnp.float32)
        act_grad = weight * lax.dot_general(
            dy, w_d[...], contract_last, preferred_element_type=jnp.float32
        )
        gate_pre, up_pre = pre[:, :half], pre[:, half:]
        sigmoid_g = jax.nn.sigmoid(gate_pre)
        swish_val = gate_pre * sigmoid_g
        acts[side, k] = (swish_val * up_pre * weight).astype(jnp.bfloat16)
        hidden[side, k, :, :half] = (
            act_grad * up_pre * sigmoid_g * (1.0 + gate_pre * (1.0 - sigmoid_g))
        ).astype(jnp.bfloat16)
        hidden[side, k, :, half:] = (act_grad * swish_val).astype(jnp.bfloat16)
        part = lax.dot_general(
            hidden[side, k], w_gu[...], contract_last, preferred_element_type=jnp.float32
        )
        part_send[side, k, 0] = part[tr : 2 * tr].astype(jnp.bfloat16)
        part_send[side, k, 1] = part[3 * tr :].astype(jnp.bfloat16)
        by_part[side, k] = send(part_send.at[side, k], part_recv.at[side, k], core_peer)
        part_own[side, k, 0] = part[:tr]
        part_own[side, k, 1] = part[2 * tr : 3 * tr]

    def add_core(side, k):
        by_part[side, k].wait_recv()
        y_send[side, k] = (
            part_own[side, k, 1] + part_recv[side, k, 1].astype(jnp.float32)
        ).astype(jnp.bfloat16)
        by_y_part[side, k] = send(y_send.at[side, k], y_recv.at[side, k], y_peer)
        part_own[side, k, 0] += part_recv[side, k, 0].astype(jnp.float32)

    def add_y(side, k):
        by_y_part[side, k].wait_recv()
        total = part_own[side, k, 0] + y_recv[side, k].astype(jnp.float32)
        if side:
            z_send[k] = total.astype(jnp.bfloat16)
            by_z_part[k] = send(z_send.at[k], z_recv.at[k], mirror)
        else:
            part_own[side, k, 0] = total

    def add_z(k):
        by_z_part[k].wait_recv()
        tok_out[pl.ds(k * tr, tr), :] = (
            part_own[0, k, 0] + z_recv[k].astype(jnp.float32)
        ).astype(jnp.bfloat16)

    tile = half
    contract_rows = (((0,), (0,)), ((), ()))

    def weight_grads(first, last):
        @pl.loop(first, last)
        def _(i):
            span = pl.ds(pl.multiple_of(i * tile, tile), tile)
            total_gu = jnp.zeros((tile, 2 * half), jnp.float32)
            total_d = jnp.zeros((half, tile), jnp.float32)
            for side in range(2):
                for k in range(chunks):
                    x = rows[side, k, 0, :, :, span].reshape(SLOTS * tr, tile)
                    dy = rows[side, k, 1, :, :, span].reshape(SLOTS * tr, tile)
                    total_gu += lax.dot_general(
                        x, hidden[side, k], contract_rows, preferred_element_type=jnp.float32
                    )
                    total_d += lax.dot_general(
                        acts[side, k], dy, contract_rows, preferred_element_type=jnp.float32
                    )
            total_gu = (total_gu * scale).astype(jnp.bfloat16)
            g_out[span, :] = total_gu[:, :half]
            u_out[span, :] = total_gu[:, half:]
            d_out[:, span] = (total_d * scale).astype(jnp.bfloat16)

    from_y(0, 0)
    for copy in local[own_copies:]:
        copy.wait()
    stage(0, 0)
    from_y(0, 1)
    from_z(0)
    add_core(0, 0)
    stage(0, 1)
    from_y(1, 0)
    add_core(0, 1)
    add_y(0, 0)
    stage(1, 0)
    from_z(1)
    add_core(1, 0)
    add_y(0, 1)
    add_y(1, 0)
    from_y(1, 1)
    stage(1, 1)
    tiles = width // tile
    weight_grads(0, tiles // 4)
    add_core(1, 1)
    weight_grads(tiles // 4, tiles // 2)
    add_y(1, 1)
    weight_grads(tiles // 2, tiles)
    add_z(0)
    add_z(1)
    for copy in sent:
        copy.wait_send()


def gathered(tokens, out_grad, expert_ids, gate_weights, w_gate, w_up, w_down):
    tok, width = tokens.shape[1:]
    topk = expert_ids.shape[2]
    half = w_gate.shape[3]
    sections = lax.axis_size("section")
    scale = 1.0 / math.sqrt(2 * topk * tok)
    tr = tok // CHUNKS
    names = jnp.arange(8, dtype=jnp.int32)[:, None, None]
    dense = jnp.sum(
        jnp.where(expert_ids[0][None] == names, gate_weights[0][None], 0.0), axis=2
    )
    lanes = -(-tok // 128) * 128
    dense = jnp.pad(dense, ((0, 0), (0, lanes - tok)))
    bf16, f32 = jnp.bfloat16, jnp.float32
    any_spec = pl.BlockSpec(memory_space=pl.ANY)
    vmem_spec = pl.BlockSpec(memory_space=pltpu.VMEM)
    copies = 12 * CHUNKS + 7
    macs = 8 * 8 * tok * width * half
    outs = pl.pallas_call(
        functools.partial(gathered_kernel, sections, scale),
        out_shape=(
            jax.ShapeDtypeStruct((tok, width), bf16),
            jax.ShapeDtypeStruct((width, half), bf16),
            jax.ShapeDtypeStruct((width, half), bf16),
            jax.ShapeDtypeStruct((half, width), bf16),
        ),
        in_specs=[any_spec] * 6,
        out_specs=(vmem_spec,) * 4,
        scratch_shapes=[
            pltpu.VMEM((2, CHUNKS, 2, SLOTS, tr, width), bf16),
            pltpu.VMEM((2, SLOTS, 8, lanes), f32),
            pltpu.VMEM((width, 2 * half), bf16),
            pltpu.VMEM((half, width), bf16),
            pltpu.VMEM((2, CHUNKS, SLOTS * tr, 2 * half), bf16),
            pltpu.VMEM((2, CHUNKS, SLOTS * tr, half), bf16),
            pltpu.VMEM((2, CHUNKS, 2, tr, width), bf16),
            pltpu.VMEM((2, CHUNKS, 2, tr, width), bf16),
            pltpu.VMEM((2, CHUNKS, 2, tr, width), f32),
            pltpu.VMEM((2, CHUNKS, tr, width), bf16),
            pltpu.VMEM((2, CHUNKS, tr, width), bf16),
            pltpu.VMEM((CHUNKS, tr, width), bf16),
            pltpu.VMEM((CHUNKS, tr, width), bf16),
            pltpu.SemaphoreType.DMA((copies,)),
            pltpu.SemaphoreType.DMA((copies,)),
            pltpu.SemaphoreType.DMA((2 * CHUNKS + 4,)),
        ],
        compiler_params=pltpu.CompilerParams(
            collective_id=0, has_side_effects=True, vmem_limit_bytes=56 * 2**20
        ),
        cost_estimate=pl.CostEstimate(
            flops=2 * macs, bytes_accessed=2**23, transcendentals=8 * tok * half
        ),
    )(tokens[0], out_grad[0], dense, w_gate[0, 0], w_up[0, 0], w_down[0, 0])
    tok_grad, out_g, out_u, out_d = outs
    return (tok_grad[None], out_g[None, None], out_u[None, None], out_d[None, None])


def solution(mesh):
    in_specs = (
        P("section", "expert", None),
        P("section", "expert", None),
        P("section", "expert", None),
        P("section", "expert", None),
        P("section", "expert", None, None),
        P("section", "expert", None, None),
        P("section", "expert", None, None),
    )
    out_specs = (
        P("section", "expert", None),
        P("section", "expert", None, None),
        P("section", "expert", None, None),
        P("section", "expert", None, None),
    )
    body = gathered if mesh.shape["expert"] == SLOTS else per_device
    return jax.shard_map(
        body, mesh=mesh, in_specs=in_specs, out_specs=out_specs, check_vma=False
    )
```
